32 devices in a mesh: leaf: 8 (over z, y), rhs: 4 (over x, core).
Axes of the slice: x: 2, y: 2, z: 4, core: 2. Of those that a mesh axis runs over, the one named last changes fastest.
Arguments:
- excitation: bfloat16 [2, 32, 65536], P(None, 'rhs', 'leaf'), parts along dimension 1, may hold values from -6 to 6
- source_weight: float32 [65536], P('leaf'), may hold values from 0.25 to 4
- tree_order: int32 [65536], P('leaf'), may hold values from 0 to 8191, as said below
- leaf_basis: bfloat16 [2, 64, 64], replicated, may hold values from -0.5 to 0.5
- transfer: bfloat16 [10, 2, 2, 64, 2, 64], replicated, may hold values from -0.375 to 0.375
- eval_basis: bfloat16 [2, 64, 64], replicated, may hold values from -0.5 to 0.5
Outputs:
- out_field: float32 [2, 32, 65536], P(None, 'rhs', 'leaf'), parts along dimension 1
The draws below stay inside these ranges and needn't reach their ends.
There are 4 independent parts, one for each index of `rhs`. The reference program is written for one: setup_inputs(seed, part) draws one part's arguments, and reference() takes and returns one part's arrays. A program takes and returns all parts, laid end to end along the dimension named above; an argument that names none is the same for every part. Nothing has to cross between parts.
Inputs may be any that keep to these rules, and one draw needn't show every extreme that they name: `tree_order`: each aligned block of 8192 entries (the points of one device) holds every number 0 to 8191 once.
All inputs are finite; a program needn't handle non-finite values.
Results may differ from the reference program's by a relative error of at most 0.015.
Values may be sent and summed in bfloat16 or wider, within the bound.
A program may use at most 64 MiB of HBM per device.

```python
import math
import jax
import jax.numpy as jnp
from jax import lax

R = 64
LEAF = 64
VEC = 8
LB = 7
XL = 3
LEVELS = 10
PTS_DEV = 8192
PTS = 65536


def draw_tree_order(key, part):
    key = jax.random.fold_in(key, 11)
    keys_all = jax.random.split(key, PTS // PTS_DEV)
    blocks = jax.vmap(lambda one_key: jax.random.permutation(one_key, PTS_DEV))(keys_all)
    return blocks.reshape(-1).astype(jnp.int32)


def block_scale(rng, extent, cuts, least, high):
    loudness = 1.0
    for position, blocks in cuts:
        draws = jax.random.uniform(jax.random.fold_in(jax.random.fold_in(rng, 6), position), (blocks,), jnp.float32, least / len(cuts), high / len(cuts))
        loudness = loudness * jnp.repeat(jnp.exp(draws), extent[position] // blocks).reshape((-1,) + (1,) * (len(extent) - 1 - position))
    return loudness


def noise(rng, dims, spread, most, cuts=(), kind=jnp.bfloat16):
    entries = spread * jax.random.normal(rng, dims, jnp.float32)
    if cuts:
        entries = entries * block_scale(rng, dims, cuts, -0.22, 0.18)
    return jnp.clip(entries, -most, most).astype(kind)


def setup_inputs(seed: int = 0, part: int = 0) -> dict:
    key_list = jax.random.split(jax.random.key(seed), 7)
    own_keys = jax.random.split(jax.random.fold_in(key_list[6], part), 7)
    excitation = noise(own_keys[0], (2, VEC, PTS), 1.0, 6.0, ((2, 8),))
    source_weight = jnp.clip(jnp.exp(math.log(4.0) - 2.7725887 * jax.random.uniform(key_list[1], (PTS,), jnp.float32) ** block_scale(key_list[1], (PTS,), ((0, 8),), -0.2, 0.2)), 0.25, 4.0)
    tree_order = draw_tree_order(jax.random.fold_in(key_list[6], 71), part)
    leaf_basis = noise(key_list[3], (2, R, LEAF), (2 * LEAF) ** -0.5, 0.5)
    transfer = noise(key_list[4], (LEVELS, 2, 2, R, 2, R), (4 * R) ** -0.5, 0.375)
    eval_basis = noise(key_list[5], (2, LEAF, R), (2 * R) ** -0.5, 0.5)
    return dict(excitation=excitation, source_weight=source_weight, tree_order=tree_order, leaf_basis=leaf_basis, transfer=transfer, eval_basis=eval_basis)


def complex_form(blocks_pair):
    real_part = blocks_pair[0].astype(jnp.float32)
    imag_part = blocks_pair[1].astype(jnp.float32)
    return jnp.stack([jnp.stack([real_part, -imag_part]), jnp.stack([imag_part, real_part])])


def merge_level(coeffs, matrix, sources, targets, vec_width):
    blocks = coeffs.reshape(2, coeffs.shape[1], sources // 2, 2, targets, vec_width).astype(jnp.float32)
    result = jnp.einsum("pqjrey,qysetv->prstjv", complex_form(matrix), blocks, precision=lax.Precision.HIGHEST)
    return result.reshape(2, coeffs.shape[1], -1).astype(jnp.bfloat16)


def reference(excitation, source_weight, tree_order, leaf_basis, transfer, eval_basis):
    point_count = excitation.shape[2]
    box_count = point_count // LEAF
    offsets = (jnp.arange(point_count, dtype=jnp.int32) // PTS_DEV) * PTS_DEV
    tree_points = (offsets + tree_order).astype(jnp.int32)
    weighted = (excitation[:, :, tree_points].astype(jnp.float32) * source_weight[tree_points]).astype(jnp.bfloat16)
    leaf_boxes = weighted.reshape(2, VEC, box_count, LEAF).astype(jnp.float32)
    coeffs = jnp.einsum("pqrl,qvsl->prsv", complex_form(leaf_basis), leaf_boxes, precision=lax.Precision.HIGHEST)
    coeffs = coeffs.reshape(2, R, box_count * VEC).astype(jnp.bfloat16)
    for level_index in range(LB + XL):
        coeffs = merge_level(coeffs, transfer[level_index], box_count >> level_index, 1 << level_index, VEC)
    grouped = coeffs.reshape(2, R, box_count, VEC).astype(jnp.float32)
    values = jnp.einsum("pqlr,qrtv->pvtl", complex_form(eval_basis), grouped, precision=lax.Precision.HIGHEST)
    potential = values.reshape(2, VEC, point_count)
    return jnp.zeros((2, VEC, point_count), jnp.float32).at[:, :, tree_points].set(potential)
```

```python
import functools
import jax
import jax.numpy as jnp
from jax import lax
from jax.experimental import pallas as pl
from jax.experimental.pallas import tpu as pltpu
from jax.sharding import PartitionSpec as P

LANES = 256
VMEM_BYTES = 48 * 1024 * 1024


def dot_rows(left, right):
    return lax.dot_general(
        left, right, (((1,), (1,)), ((), ())), preferred_element_type=jnp.float32
    )


def level_matrix(transfer_ref, level):
    rank = transfer_ref.shape[3]
    rows = []
    for child in range(2):
        real = transfer_ref[level, 0, child]
        imag = transfer_ref[level, 1, child]
        real_0, real_1 = real[:, :rank], real[:, rank:]
        imag_0, imag_1 = imag[:, :rank], imag[:, rank:]
        rows.append(jnp.concatenate([real_0, -imag_0, real_1, -imag_1], axis=1))
        rows.append(jnp.concatenate([imag_0, real_0, imag_1, real_1], axis=1))
    return jnp.concatenate(rows, axis=0)


def leaf_matrix(basis_ref):
    real, imag = basis_ref[0], basis_ref[1]
    zero = jnp.zeros_like(real)
    rows = [
        jnp.concatenate([real, zero, -imag, zero], axis=1),
        jnp.concatenate([imag, zero, real, zero], axis=1),
        jnp.concatenate([zero, real, zero, -imag], axis=1),
        jnp.concatenate([zero, imag, zero, real], axis=1),
    ]
    return jnp.concatenate(rows, axis=0)


def eval_matrix(basis_ref):
    real, imag = basis_ref[0], basis_ref[1]
    zero = jnp.zeros_like(real)
    rows = [
        jnp.concatenate([real, -imag, zero, zero], axis=1),
        jnp.concatenate([zero, zero, real, -imag], axis=1),
        jnp.concatenate([imag, real, zero, zero], axis=1),
        jnp.concatenate([zero, zero, imag, real], axis=1),
    ]
    return jnp.concatenate(rows, axis=0)


def pair_up(state, targets, vecs):
    rows, width = state.shape
    block = targets * vecs
    if block % 16:
        state = state.astype(jnp.float32)
    split = state.reshape(rows // (2 * block), 2, block, width)
    joined = jnp.concatenate([split[:, 0], split[:, 1]], axis=-1)
    return joined.reshape(rows // 2, 2 * width).astype(jnp.bfloat16)


def children(result, vecs):
    rows, width = result.shape
    half = width // 2
    blocks = result.reshape(rows // vecs, vecs, width)
    stacked = jnp.stack([blocks[..., :half], blocks[..., half:]], axis=1)
    return stacked.reshape(rows * 2, half).astype(jnp.bfloat16)


def one_hot(order_block):
    low = jnp.bitwise_and(order_block, LANES - 1)
    rows = lax.broadcasted_iota(jnp.int32, (LANES, order_block.shape[1]), 0)
    return jnp.where(rows == low, 1.0, 0.0).astype(jnp.bfloat16)


def near_kernel(local_levels, exc_ref, weight_ref, order_ref, leaf_ref, transfer_ref,
                out_ref, weighted, pairs):
    vecs = exc_ref.shape[1]
    points = exc_ref.shape[2]
    blocks = points // LANES
    half = LANES // 2
    for block in range(blocks):
        lanes = pl.ds(block * LANES, LANES)
        scaled = [
            exc_ref[part, :, lanes].astype(jnp.float32) * weight_ref[:, lanes] for part in range(2)
        ]
        weighted[pl.ds(block * 2 * vecs, 2 * vecs), :] = jnp.concatenate(scaled, axis=0).astype(
            jnp.bfloat16
        )

    def gather(step, carry):
        order = order_ref[:, pl.ds(pl.multiple_of(step * LANES, LANES), LANES)]
        spread = jnp.dot(weighted[...], one_hot(order), preferred_element_type=jnp.float32)
        high = jnp.broadcast_to(lax.shift_right_logical(order, 8), (2 * vecs, LANES))
        picked = spread[: 2 * vecs]
        for block in range(1, blocks):
            picked = jnp.where(
                high == block, spread[block * 2 * vecs : (block + 1) * 2 * vecs], picked
            )
        rows = [
            jnp.concatenate([picked[:vecs, lo : lo + half], picked[vecs:, lo : lo + half]], axis=1)
            for lo in (0, half)
        ]
        pairs[pl.ds(pl.multiple_of(step * 2 * vecs, 2 * vecs), 2 * vecs), :] = jnp.concatenate(
            rows, axis=0
        ).astype(jnp.bfloat16)
        return carry

    lax.fori_loop(0, blocks, gather, 0, unroll=2)
    joined = dot_rows(pairs[...], leaf_matrix(leaf_ref)).astype(jnp.bfloat16)
    for level in range(local_levels):
        result = dot_rows(joined, level_matrix(transfer_ref, level))
        state = children(result, vecs)
        if level + 1 < local_levels:
            joined = pair_up(state, 2 << level, vecs)
    out_ref[...] = state


def far_kernel(local_levels, per_peer, vecs, state_ref, order_ref, transfer_ref, eval_ref,
               out_ref, values, total):
    levels = transfer_ref.shape[0]
    points = order_ref.shape[1]
    blocks = points // LANES
    half = LANES // 2
    state = state_ref[...]
    targets = per_peer
    for level in range(local_levels, levels):
        result = dot_rows(pair_up(state, targets, vecs), level_matrix(transfer_ref, level))
        state = children(result, vecs)
        targets *= 2
    joined = pair_up(state, 1, vecs)
    values[...] = dot_rows(joined, eval_matrix(eval_ref))
    total[...] = jnp.zeros_like(total)

    def scatter(step, carry):
        order = order_ref[:, pl.ds(pl.multiple_of(step * LANES, LANES), LANES)]
        held = values[pl.ds(pl.multiple_of(step * 2 * vecs, 2 * vecs), 2 * vecs), :]
        block_values = jnp.concatenate(
            [
                jnp.concatenate([held[:vecs, lo : lo + half], held[vecs:, lo : lo + half]], axis=1)
                for lo in (0, half)
            ],
            axis=0,
        )
        high = jnp.broadcast_to(lax.shift_right_logical(order, 8), (2 * vecs, LANES))
        spread = jnp.concatenate(
            [jnp.where(high == block, block_values, 0.0).astype(jnp.bfloat16) for block in range(blocks)],
            axis=0,
        )
        total[...] += dot_rows(spread, one_hot(order))
        return carry

    lax.fori_loop(0, blocks, scatter, 0, unroll=2)
    for block in range(blocks):
        rows = block * 2 * vecs
        for part in range(2):
            out_ref[part, :, pl.ds(block * LANES, LANES)] = total[
                pl.ds(rows + part * vecs, vecs), :
            ]


def per_device(excitation, source_weight, tree_order, leaf_basis, transfer, eval_basis):
    vecs, points = excitation.shape[1:]
    levels, rank = transfer.shape[0], leaf_basis.shape[1]
    leaf_size = leaf_basis.shape[2]
    boxes = points // leaf_size
    count = lax.axis_size("leaf")
    cross_levels = count.bit_length() - 1
    local_levels = levels - cross_levels
    per_peer = boxes // count
    transfer = transfer.reshape(levels, 2, 2, rank, 2 * rank)
    weight_row = source_weight.reshape(1, points)
    order_row = tree_order.reshape(1, points)
    params = pltpu.CompilerParams(vmem_limit_bytes=VMEM_BYTES)
    wide = points // LANES * 2 * vecs
    state = pl.pallas_call(
        functools.partial(near_kernel, local_levels),
        out_shape=jax.ShapeDtypeStruct((boxes * vecs, 2 * rank), jnp.bfloat16),
        scratch_shapes=[
            pltpu.VMEM((wide, LANES), jnp.bfloat16),
            pltpu.VMEM((boxes * vecs // 2, 4 * rank), jnp.bfloat16),
        ],
        compiler_params=params,
        name="near",
    )(excitation, weight_row, order_row, leaf_basis, transfer)
    state = lax.all_to_all(state, "leaf", split_axis=0, concat_axis=0, tiled=True)
    return pl.pallas_call(
        functools.partial(far_kernel, local_levels, per_peer, vecs),
        out_shape=jax.ShapeDtypeStruct((2, vecs, points), jnp.float32),
        scratch_shapes=[
            pltpu.VMEM((boxes * vecs // 2, 4 * rank), jnp.float32),
            pltpu.VMEM((wide, LANES), jnp.float32),
        ],
        compiler_params=params,
        name="far",
    )(state, order_row, transfer, eval_basis)


def solution(mesh):
    in_specs = (P(None, "rhs", "leaf"), P("leaf"), P("leaf"), P(), P(), P())
    return jax.shard_map(
        per_device, mesh=mesh, in_specs=in_specs, out_specs=P(None, "rhs", "leaf"), check_vma=False
    )
```

```python
import functools
import jax
import jax.numpy as jnp
from jax import lax
from jax.experimental import pallas as pl
from jax.experimental.pallas import tpu as pltpu
from jax.sharding import PartitionSpec as P

LANES = 256
CHUNKS = 2
VMEM_BYTES = 56 * 1024 * 1024


def dot_rows(left, right):
    return lax.dot_general(
        left, right, (((1,), (1,)), ((), ())), preferred_element_type=jnp.float32
    )


def level_matrix(transfer_ref, level, halves):
    rank = transfer_ref.shape[4]
    for part in range(2):
        for child in range(2):
            halves[part, child] = transfer_ref[level, part, child].astype(jnp.float32)
    rows = []
    for child in range(2):
        real_0, real_1 = (halves[0, child, pl.ds(half, rank, stride=2), :] for half in range(2))
        imag_0, imag_1 = (halves[1, child, pl.ds(half, rank, stride=2), :] for half in range(2))
        rows.append(jnp.concatenate([real_0, -imag_0, real_1, -imag_1], axis=1))
        rows.append(jnp.concatenate([imag_0, real_0, imag_1, real_1], axis=1))
    return jnp.concatenate(rows, axis=0).astype(jnp.bfloat16)


def leaf_matrix(basis_ref):
    real, imag = basis_ref[0], basis_ref[1]
    zero = jnp.zeros_like(real)
    rows = [
        jnp.concatenate([real, zero, -imag, zero], axis=1),
        jnp.concatenate([imag, zero, real, zero], axis=1),
        jnp.concatenate([zero, real, zero, -imag], axis=1),
        jnp.concatenate([zero, imag, zero, real], axis=1),
    ]
    return jnp.concatenate(rows, axis=0)


def eval_matrix(basis_ref):
    real, imag = basis_ref[0], basis_ref[1]
    zero = jnp.zeros_like(real)
    rows = [
        jnp.concatenate([real, -imag, zero, zero], axis=1),
        jnp.concatenate([zero, zero, real, -imag], axis=1),
        jnp.concatenate([imag, real, zero, zero], axis=1),
        jnp.concatenate([zero, zero, imag, real], axis=1),
    ]
    return jnp.concatenate(rows, axis=0)


def pair_up(state, targets, vecs):
    rows, width = state.shape
    block = targets * vecs
    if block % 16:
        state = state.astype(jnp.float32)
    split = state.reshape(rows // (2 * block), 2, block, width)
    joined = jnp.concatenate([split[:, 0], split[:, 1]], axis=-1)
    return joined.reshape(rows // 2, 2 * width).astype(jnp.bfloat16)


def children(result, vecs):
    rows, width = result.shape
    half = width // 2
    blocks = result.reshape(rows // vecs, vecs, width)
    stacked = jnp.stack([blocks[..., :half], blocks[..., half:]], axis=1)
    return stacked.reshape(rows * 2, half).astype(jnp.bfloat16)


def one_hot(order_block):
    low = jnp.bitwise_and(order_block, LANES - 1)
    rows = lax.broadcasted_iota(jnp.int32, (LANES, order_block.shape[1]), 0)
    return jnp.where(rows == low, 1.0, 0.0).astype(jnp.bfloat16)


def aligned(index, size):
    return pl.ds(pl.multiple_of(index * size, size), size)


def weigh(exc_ref, weight_ref, weighted):
    vecs, points = exc_ref.shape[1:]
    for block in range(points // LANES):
        lanes = pl.ds(block * LANES, LANES)
        scaled = [
            exc_ref[part, :, lanes].astype(jnp.float32) * weight_ref[:, lanes] for part in range(2)
        ]
        weighted[pl.ds(block * 2 * vecs, 2 * vecs), :] = jnp.concatenate(scaled, axis=0).astype(
            jnp.bfloat16
        )


def gather_step(step, vecs, blocks, order_ref, weighted, hot, pairs):
    half = LANES // 2
    order = order_ref[:, aligned(step, LANES)]
    table = one_hot(order)
    hot[step] = table
    spread = jnp.dot(weighted[...], table, preferred_element_type=jnp.float32)
    high = jnp.broadcast_to(lax.shift_right_logical(order, 8), (vecs, LANES))
    real, imag = spread[:vecs], spread[vecs : 2 * vecs]
    for block in range(1, blocks):
        here = high == block
        base = block * 2 * vecs
        real = jnp.where(here, spread[base : base + vecs], real)
        imag = jnp.where(here, spread[base + vecs : base + 2 * vecs], imag)
    rows = [
        jnp.concatenate([real[:, lo : lo + half], imag[:, lo : lo + half]], axis=1)
        for lo in (0, half)
    ]
    pairs[aligned(step, 2 * vecs), :] = jnp.concatenate(rows, axis=0).astype(jnp.bfloat16)


def scatter_steps(group, vecs, blocks, count, order_ref, hot, values, total):
    half = LANES // 2
    spreads, tables = [], []
    for inner in range(count):
        step = group * count + inner
        order = order_ref[:, aligned(step, LANES)]
        held = values[aligned(step, 2 * vecs), :]
        real, imag = (
            jnp.concatenate([held[:vecs, lo : lo + half], held[vecs:, lo : lo + half]], axis=1)
            for lo in (0, half)
        )
        high = jnp.broadcast_to(lax.shift_right_logical(order, 8), (vecs, LANES))
        rows = []
        for block in range(blocks):
            here = high == block
            rows.append(jnp.where(here, real, 0.0))
            rows.append(jnp.where(here, imag, 0.0))
        spreads.append(jnp.concatenate(rows, axis=0).astype(jnp.bfloat16))
        tables.append(hot[step])
    total[...] += dot_rows(jnp.concatenate(spreads, axis=1), jnp.concatenate(tables, axis=1))


def write_out(vecs, blocks, total, out_ref):
    for block in range(blocks):
        rows = block * 2 * vecs
        for part in range(2):
            out_ref[part, :, pl.ds(block * LANES, LANES)] = total[
                pl.ds(rows + part * vecs, vecs), :
            ]


def fused_kernel(count, chunks, near_levels, exc_ref, weight_ref, order_ref, leaf_ref, transfer_ref,
                 eval_ref, out_ref, weighted, pairs, hot, mats, halves, sent, held, values, total,
                 send_sems, recv_sems):
    vecs, points = exc_ref.shape[1:]
    levels = transfer_ref.shape[0]
    blocks = points // LANES
    me = lax.axis_index("leaf")
    peers = [(hop, lax.rem(me + hop, count)) for hop in range(1, count)]
    barrier = pltpu.get_barrier_semaphore()
    for hop, peer in peers:
        pl.semaphore_signal(
            barrier, inc=1, device_id={"leaf": peer}, device_id_type=pl.DeviceIdType.MESH
        )
    weigh(exc_ref, weight_ref, weighted)
    for level in range(near_levels):
        mats[level] = level_matrix(transfer_ref, level, halves)
    mats[levels] = leaf_matrix(leaf_ref)
    steps = blocks // chunks
    rows = sent.shape[2]
    copies = []
    for chunk in range(chunks):

        def gather(step, carry):
            gather_step(chunk * steps + step, vecs, blocks, order_ref, weighted, hot, pairs)
            return carry

        lax.fori_loop(0, steps, gather, 0, unroll=2)
        start = chunk * steps * 2 * vecs
        joined = dot_rows(pairs[start : start + steps * 2 * vecs, :], mats[levels]).astype(
            jnp.bfloat16
        )
        for level in range(near_levels):
            state = children(dot_rows(joined, mats[level]), vecs)
            if level + 1 < near_levels:
                joined = pair_up(state, 2 << level, vecs)
        sent[chunk] = state.reshape(count, rows, state.shape[1])
        if chunk == 0:
            pl.semaphore_wait(barrier, count - 1)
        for hop, peer in peers:
            copy = pltpu.make_async_remote_copy(
                src_ref=sent.at[chunk, peer],
                dst_ref=held.at[me * chunks + chunk],
                send_sem=send_sems.at[chunk, hop],
                recv_sem=recv_sems.at[chunk, hop],
                device_id={"leaf": peer},
                device_id_type=pl.DeviceIdType.MESH,
            )
            copy.start()
            copies.append(copy)
        held[me * chunks + chunk] = sent[chunk, me]
    for level in range(near_levels, levels):
        mats[level] = level_matrix(transfer_ref, level, halves)
    mats[levels + 1] = eval_matrix(eval_ref)
    total[...] = jnp.zeros_like(total)
    for copy in copies:
        copy.wait()
    state = held[...].reshape(count * chunks * rows, held.shape[2])
    targets = rows // vecs
    for level in range(near_levels, levels):
        state = children(dot_rows(pair_up(state, targets, vecs), mats[level]), vecs)
        targets *= 2
    values[...] = dot_rows(pair_up(state, 1, vecs), mats[levels + 1])
    group = 2

    def scatter(step, carry):
        scatter_steps(step, vecs, blocks, group, order_ref, hot, values, total)
        return carry

    lax.fori_loop(0, blocks // group, scatter, 0)
    write_out(vecs, blocks, total, out_ref)


def near_kernel(near_levels, exc_ref, weight_ref, order_ref, leaf_ref, transfer_ref,
                out_ref, weighted, hot, pairs, halves):
    vecs, points = exc_ref.shape[1:]
    blocks = points // LANES
    weigh(exc_ref, weight_ref, weighted)

    def gather(step, carry):
        gather_step(step, vecs, blocks, order_ref, weighted, hot, pairs)
        return carry

    lax.fori_loop(0, blocks, gather, 0)
    joined = dot_rows(pairs[...], leaf_matrix(leaf_ref)).astype(jnp.bfloat16)
    for level in range(near_levels):
        state = children(dot_rows(joined, level_matrix(transfer_ref, level, halves)), vecs)
        if level + 1 < near_levels:
            joined = pair_up(state, 2 << level, vecs)
    out_ref[...] = state


def far_kernel(near_levels, per_peer, vecs, state_ref, order_ref, transfer_ref, eval_ref,
               out_ref, hot, values, total, halves):
    blocks = order_ref.shape[1] // LANES
    state = state_ref[...]
    targets = per_peer
    for level in range(near_levels, transfer_ref.shape[0]):
        matrix = level_matrix(transfer_ref, level, halves)
        state = children(dot_rows(pair_up(state, targets, vecs), matrix), vecs)
        targets *= 2
    values[...] = dot_rows(pair_up(state, 1, vecs), eval_matrix(eval_ref))
    total[...] = jnp.zeros_like(total)

    def scatter(step, carry):
        hot[step] = one_hot(order_ref[:, aligned(step, LANES)])
        scatter_steps(step, vecs, blocks, 1, order_ref, hot, values, total)
        return carry

    lax.fori_loop(0, blocks, scatter, 0)
    write_out(vecs, blocks, total, out_ref)


def per_device(excitation, source_weight, tree_order, leaf_basis, transfer, eval_basis):
    vecs, points = excitation.shape[1:]
    levels, rank = transfer.shape[0], leaf_basis.shape[1]
    leaf_size = leaf_basis.shape[2]
    boxes = points // leaf_size
    blocks = points // LANES
    count = lax.axis_size("leaf")
    transfer = transfer.reshape(levels, 2, 2, 2 * rank, rank)
    weight_row = source_weight.reshape(1, points)
    order_row = tree_order.reshape(1, points)
    box_levels = boxes.bit_length() - 1
    out_shape = jax.ShapeDtypeStruct((2, vecs, points), jnp.float32)
    weighted = pltpu.VMEM((blocks * 2 * vecs, LANES), jnp.bfloat16)
    pairs = pltpu.VMEM((boxes * vecs // 2, 4 * rank), jnp.bfloat16)
    values = pltpu.VMEM((boxes * vecs // 2, 4 * rank), jnp.float32)
    total = pltpu.VMEM((blocks * 2 * vecs, LANES), jnp.float32)
    hot = pltpu.VMEM((blocks, LANES, LANES), jnp.bfloat16)
    halves = pltpu.VMEM((2, 2, 2 * rank, rank), jnp.float32)
    chunks = CHUNKS
    while chunks > 1 and boxes // chunks // count * vecs < 16:
        chunks //= 2
    rows = boxes // chunks // count * vecs
    if rows >= 16:
        near_levels = box_levels - (chunks.bit_length() - 1)
        return pl.pallas_call(
            functools.partial(fused_kernel, count, chunks, near_levels),
            out_shape=out_shape,
            in_specs=[pl.BlockSpec(memory_space=pltpu.VMEM)] * 6,
            out_specs=pl.BlockSpec(memory_space=pltpu.VMEM),
            scratch_shapes=[
                weighted,
                pairs,
                hot,
                pltpu.VMEM((levels + 2, 4 * rank, 4 * rank), jnp.bfloat16),
                halves,
                pltpu.VMEM((chunks, count, rows, 2 * rank), jnp.bfloat16),
                pltpu.VMEM((count * chunks, rows, 2 * rank), jnp.bfloat16),
                values,
                total,
                pltpu.SemaphoreType.DMA((chunks, count)),
                pltpu.SemaphoreType.DMA((chunks, count)),
            ],
            compiler_params=pltpu.CompilerParams(
                vmem_limit_bytes=VMEM_BYTES, collective_id=0, has_side_effects=True
            ),
            name="fused",
        )(excitation, weight_row, order_row, leaf_basis, transfer, eval_basis)
    params = pltpu.CompilerParams(vmem_limit_bytes=VMEM_BYTES)
    state = pl.pallas_call(
        functools.partial(near_kernel, box_levels),
        out_shape=jax.ShapeDtypeStruct((boxes * vecs, 2 * rank), jnp.bfloat16),
        scratch_shapes=[weighted, hot, pairs, halves],
        compiler_params=params,
        name="near",
    )(excitation, weight_row, order_row, leaf_basis, transfer)
    state = lax.all_to_all(state, "leaf", split_axis=0, concat_axis=0, tiled=True)
    return pl.pallas_call(
        functools.partial(far_kernel, box_levels, boxes // count, vecs),
        out_shape=out_shape,
        scratch_shapes=[hot, values, total, halves],
        compiler_params=params,
        name="far",
    )(state, order_row, transfer, eval_basis)


def solution(mesh):
    in_specs = (P(None, "rhs", "leaf"), P("leaf"), P("leaf"), P(), P(), P())
    return jax.shard_map(
        per_device, mesh=mesh, in_specs=in_specs, out_specs=P(None, "rhs", "leaf"), check_vma=False
    )
```

```python
import functools
import jax
import jax.numpy as jnp
from jax import lax
from jax.experimental import pallas as pl
from jax.experimental.pallas import tpu as pltpu
from jax.sharding import PartitionSpec as P

LANES = 256
CHUNKS = 2
UNROLL = 8
GROUP = 8
SPLIT_BYTES = 32 * 1024 * 1024
VMEM_BYTES = 56 * 1024 * 1024


def dot_rows(left, right):
    return lax.dot_general(
        left, right, (((1,), (1,)), ((), ())), preferred_element_type=jnp.float32
    )


def level_matrix(transfer_ref, level, halves):
    rank = transfer_ref.shape[4]
    for part in range(2):
        for child in range(2):
            halves[part, child] = transfer_ref[level, part, child].astype(jnp.float32)
    rows = []
    for child in range(2):
        real_0, real_1 = (halves[0, child, pl.ds(half, rank, stride=2), :] for half in range(2))
        imag_0, imag_1 = (halves[1, child, pl.ds(half, rank, stride=2), :] for half in range(2))
        rows.append(jnp.concatenate([real_0, -imag_0, real_1, -imag_1], axis=1))
        rows.append(jnp.concatenate([imag_0, real_0, imag_1, real_1], axis=1))
    return jnp.concatenate(rows, axis=0).astype(jnp.bfloat16)


def leaf_matrix(basis_ref):
    real, imag = basis_ref[0], basis_ref[1]
    zero = jnp.zeros_like(real)
    rows = [
        jnp.concatenate([real, zero, -imag, zero], axis=1),
        jnp.concatenate([imag, zero, real, zero], axis=1),
        jnp.concatenate([zero, real, zero, -imag], axis=1),
        jnp.concatenate([zero, imag, zero, real], axis=1),
    ]
    return jnp.concatenate(rows, axis=0)


def eval_matrix(basis_ref):
    real, imag = basis_ref[0], basis_ref[1]
    zero = jnp.zeros_like(real)
    rows = [
        jnp.concatenate([real, -imag, zero, zero], axis=1),
        jnp.concatenate([zero, zero, real, -imag], axis=1),
        jnp.concatenate([imag, real, zero, zero], axis=1),
        jnp.concatenate([zero, zero, imag, real], axis=1),
    ]
    return jnp.concatenate(rows, axis=0)


def pair_up(state, targets, vecs):
    rows, width = state.shape
    block = targets * vecs
    if block % 16:
        state = state.astype(jnp.float32)
    split = state.reshape(rows // (2 * block), 2, block, width)
    joined = jnp.concatenate([split[:, 0], split[:, 1]], axis=-1)
    return joined.reshape(rows // 2, 2 * width).astype(jnp.bfloat16)


def children(result, vecs):
    rows, width = result.shape
    half = width // 2
    blocks = result.reshape(rows // vecs, vecs, width)
    stacked = jnp.stack([blocks[..., :half], blocks[..., half:]], axis=1)
    return stacked.reshape(rows * 2, half).astype(jnp.bfloat16)


def one_hot(order_block):
    low = jnp.bitwise_and(order_block, LANES - 1)
    rows = lax.broadcasted_iota(jnp.int32, (LANES, order_block.shape[1]), 0)
    return jnp.where(rows == low, 1.0, 0.0).astype(jnp.bfloat16)


def aligned(index, size):
    return pl.ds(pl.multiple_of(index * size, size), size)


def weigh(exc_ref, weight_ref, weighted):
    vecs, points = exc_ref.shape[1:]
    for block in range(points // LANES):
        lanes = pl.ds(block * LANES, LANES)
        scaled = [
            exc_ref[part, :, lanes].astype(jnp.float32) * weight_ref[:, lanes] for part in range(2)
        ]
        weighted[pl.ds(block * 2 * vecs, 2 * vecs), :] = jnp.concatenate(scaled, axis=0).astype(
            jnp.bfloat16
        )


def gather_step(step, vecs, blocks, order_ref, weighted, hot, pairs):
    half = LANES // 2
    order = order_ref[:, aligned(step, LANES)]
    table = one_hot(order)
    hot[step] = table
    spread = jnp.dot(weighted[...], table, preferred_element_type=jnp.float32)
    high = jnp.broadcast_to(lax.shift_right_logical(order, 8), (vecs, LANES))
    real, imag = spread[:vecs], spread[vecs : 2 * vecs]
    for block in range(1, blocks):
        here = high == block
        base = block * 2 * vecs
        real = jnp.where(here, spread[base : base + vecs], real)
        imag = jnp.where(here, spread[base + vecs : base + 2 * vecs], imag)
    rows = [
        jnp.concatenate([real[:, lo : lo + half], imag[:, lo : lo + half]], axis=1)
        for lo in (0, half)
    ]
    pairs[aligned(step, 2 * vecs), :] = jnp.concatenate(rows, axis=0).astype(jnp.bfloat16)


def scatter_steps(group, vecs, blocks, count, order_ref, hot, values, total):
    half = LANES // 2
    spreads, tables = [], []
    for inner in range(count):
        step = group * count + inner
        order = order_ref[:, aligned(step, LANES)]
        held = values[aligned(step, 2 * vecs), :]
        real, imag = (
            jnp.concatenate([held[:vecs, lo : lo + half], held[vecs:, lo : lo + half]], axis=1)
            for lo in (0, half)
        )
        high = jnp.broadcast_to(lax.shift_right_logical(order, 8), (vecs, LANES))
        rows = []
        for block in range(blocks):
            here = high == block
            rows.append(jnp.where(here, real, 0.0))
            rows.append(jnp.where(here, imag, 0.0))
        spreads.append(jnp.concatenate(rows, axis=0).astype(jnp.bfloat16))
        tables.append(hot[step])
    total[...] += dot_rows(jnp.concatenate(spreads, axis=1), jnp.concatenate(tables, axis=1))


def write_out(vecs, blocks, total, out_ref):
    for block in range(blocks):
        rows = block * 2 * vecs
        for part in range(2):
            out_ref[part, :, pl.ds(block * LANES, LANES)] = total[
                pl.ds(rows + part * vecs, vecs), :
            ]


def send_kernel(count, chunks, near_levels, unroll, exc_ref, weight_ref, order_ref, leaf_ref,
                transfer_ref, eval_ref, held, hot, far_mats, weighted, pairs, mats, halves, sent,
                send_sems, recv_sems):
    vecs, points = exc_ref.shape[1:]
    levels = transfer_ref.shape[0]
    blocks = points // LANES
    me = lax.axis_index("leaf")
    peers = [(hop, lax.rem(me + hop, count)) for hop in range(1, count)]
    barrier = pltpu.get_barrier_semaphore()
    for hop, peer in peers:
        pl.semaphore_signal(
            barrier, inc=1, device_id={"leaf": peer}, device_id_type=pl.DeviceIdType.MESH
        )
    weigh(exc_ref, weight_ref, weighted)
    for level in range(near_levels):
        mats[level] = level_matrix(transfer_ref, level, halves)
    mats[near_levels] = leaf_matrix(leaf_ref)
    steps = blocks // chunks
    sources, rows, width = held.shape[1:]
    sources //= chunks
    copies = []
    for chunk in range(chunks):

        def gather(step, carry):
            gather_step(chunk * steps + step, vecs, blocks, order_ref, weighted, hot, pairs)
            return carry

        lax.fori_loop(0, steps, gather, 0, unroll=min(unroll, steps))
        start = chunk * steps * 2 * vecs
        joined = dot_rows(pairs[start : start + steps * 2 * vecs, :], mats[near_levels]).astype(
            jnp.bfloat16
        )
        for level in range(near_levels):
            state = children(dot_rows(joined, mats[level]), vecs)
            if level + 1 < near_levels:
                joined = pair_up(state, 2 << level, vecs)
        state = state.reshape(sources, count, rows, width)
        for peer in range(count):
            sent[chunk, peer] = state[:, peer]
        if chunk == 0:
            pl.semaphore_wait(barrier, count - 1)
        for hop, peer in peers:
            copy = pltpu.make_async_remote_copy(
                src_ref=sent.at[chunk, peer],
                dst_ref=held.at[me, pl.ds(chunk * sources, sources)],
                send_sem=send_sems.at[chunk, hop],
                recv_sem=recv_sems.at[chunk, hop],
                device_id={"leaf": peer},
                device_id_type=pl.DeviceIdType.MESH,
            )
            copy.start()
            copies.append(copy)
        held[me, chunk * sources : (chunk + 1) * sources] = sent[chunk, me]
    for level in range(near_levels, levels):
        far_mats[level - near_levels] = level_matrix(transfer_ref, level, halves)
    far_mats[levels - near_levels] = eval_matrix(eval_ref)
    for copy in copies:
        copy.wait()


def merge_kernel(vecs, group, held, hot, far_mats, order_ref, out_ref, values, total):
    blocks = order_ref.shape[1] // LANES
    count, sources, rows, width = held.shape
    targets = rows // vecs
    far_levels = far_mats.shape[0] - 1
    state = held[...].reshape(count * sources * rows, width)
    for level in range(far_levels):
        state = children(dot_rows(pair_up(state, targets, vecs), far_mats[level]), vecs)
        targets *= 2
    values[...] = dot_rows(pair_up(state, 1, vecs), far_mats[far_levels])
    total[...] = jnp.zeros_like(total)

    def scatter(step, carry):
        scatter_steps(step, vecs, blocks, group, order_ref, hot, values, total)
        return carry

    lax.fori_loop(0, blocks // group, scatter, 0)
    write_out(vecs, blocks, total, out_ref)


def near_kernel(near_levels, exc_ref, weight_ref, order_ref, leaf_ref, transfer_ref,
                out_ref, weighted, hot, pairs, halves):
    vecs, points = exc_ref.shape[1:]
    blocks = points // LANES
    weigh(exc_ref, weight_ref, weighted)

    def gather(step, carry):
        gather_step(step, vecs, blocks, order_ref, weighted, hot, pairs)
        return carry

    lax.fori_loop(0, blocks, gather, 0)
    joined = dot_rows(pairs[...], leaf_matrix(leaf_ref)).astype(jnp.bfloat16)
    for level in range(near_levels):
        state = children(dot_rows(joined, level_matrix(transfer_ref, level, halves)), vecs)
        if level + 1 < near_levels:
            joined = pair_up(state, 2 << level, vecs)
    out_ref[...] = state


def far_kernel(near_levels, per_peer, vecs, state_ref, order_ref, transfer_ref, eval_ref,
               out_ref, hot, values, total, halves):
    blocks = order_ref.shape[1] // LANES
    state = state_ref[...]
    targets = per_peer
    for level in range(near_levels, transfer_ref.shape[0]):
        matrix = level_matrix(transfer_ref, level, halves)
        state = children(dot_rows(pair_up(state, targets, vecs), matrix), vecs)
        targets *= 2
    values[...] = dot_rows(pair_up(state, 1, vecs), eval_matrix(eval_ref))
    total[...] = jnp.zeros_like(total)

    def scatter(step, carry):
        hot[step] = one_hot(order_ref[:, aligned(step, LANES)])
        scatter_steps(step, vecs, blocks, 1, order_ref, hot, values, total)
        return carry

    lax.fori_loop(0, blocks, scatter, 0)
    write_out(vecs, blocks, total, out_ref)


def per_device(excitation, source_weight, tree_order, leaf_basis, transfer, eval_basis):
    vecs, points = excitation.shape[1:]
    levels, rank = transfer.shape[0], leaf_basis.shape[1]
    leaf_size = leaf_basis.shape[2]
    boxes = points // leaf_size
    blocks = points // LANES
    count = lax.axis_size("leaf")
    transfer = transfer.reshape(levels, 2, 2, 2 * rank, rank)
    weight_row = source_weight.reshape(1, points)
    order_row = tree_order.reshape(1, points)
    box_levels = boxes.bit_length() - 1
    out_shape = jax.ShapeDtypeStruct((2, vecs, points), jnp.float32)
    weighted = pltpu.VMEM((blocks * 2 * vecs, LANES), jnp.bfloat16)
    pairs = pltpu.VMEM((boxes * vecs // 2, 4 * rank), jnp.bfloat16)
    values = pltpu.VMEM((boxes * vecs // 2, 4 * rank), jnp.float32)
    total = pltpu.VMEM((blocks * 2 * vecs, LANES), jnp.float32)
    hot = pltpu.VMEM((blocks, LANES, LANES), jnp.bfloat16)
    halves = pltpu.VMEM((2, 2, 2 * rank, rank), jnp.float32)
    near_levels = (16 * count // vecs).bit_length() - 1
    chunks = CHUNKS
    while chunks > 1 and boxes // chunks < 1 << near_levels:
        chunks //= 2
    if near_levels < box_levels:
        sources = boxes >> near_levels
        rows = boxes * vecs // (count * sources)
        far_count = levels - near_levels + 1
        vmem = pl.BlockSpec(memory_space=pltpu.VMEM)
        held, table, far_mats = pl.pallas_call(
            functools.partial(send_kernel, count, chunks, near_levels, UNROLL),
            out_shape=[
                jax.ShapeDtypeStruct((count, sources, rows, 2 * rank), jnp.bfloat16),
                jax.ShapeDtypeStruct((blocks, LANES, LANES), jnp.bfloat16),
                jax.ShapeDtypeStruct((far_count, 4 * rank, 4 * rank), jnp.bfloat16),
            ],
            in_specs=[vmem] * 6,
            out_specs=[vmem] * 3,
            scratch_shapes=[
                weighted,
                pairs,
                pltpu.VMEM((near_levels + 1, 4 * rank, 4 * rank), jnp.bfloat16),
                halves,
                pltpu.VMEM((chunks, count, sources // chunks, rows, 2 * rank), jnp.bfloat16),
                pltpu.SemaphoreType.DMA((chunks, count)),
                pltpu.SemaphoreType.DMA((chunks, count)),
            ],
            compiler_params=pltpu.CompilerParams(
                vmem_limit_bytes=SPLIT_BYTES, collective_id=0, has_side_effects=True
            ),
            name="send",
        )(excitation, weight_row, order_row, leaf_basis, transfer, eval_basis)
        return pl.pallas_call(
            functools.partial(merge_kernel, vecs, min(GROUP, blocks)),
            out_shape=out_shape,
            in_specs=[vmem] * 4,
            out_specs=vmem,
            scratch_shapes=[values, total],
            compiler_params=pltpu.CompilerParams(vmem_limit_bytes=SPLIT_BYTES),
            name="merge",
        )(held, table, far_mats, order_row)
    params = pltpu.CompilerParams(vmem_limit_bytes=VMEM_BYTES)
    state = pl.pallas_call(
        functools.partial(near_kernel, box_levels),
        out_shape=jax.ShapeDtypeStruct((boxes * vecs, 2 * rank), jnp.bfloat16),
        scratch_shapes=[weighted, hot, pairs, halves],
        compiler_params=params,
        name="near",
    )(excitation, weight_row, order_row, leaf_basis, transfer)
    state = lax.all_to_all(state, "leaf", split_axis=0, concat_axis=0, tiled=True)
    return pl.pallas_call(
        functools.partial(far_kernel, box_levels, boxes // count, vecs),
        out_shape=out_shape,
        scratch_shapes=[hot, values, total, halves],
        compiler_params=params,
        name="far",
    )(state, order_row, transfer, eval_basis)


def solution(mesh):
    in_specs = (P(None, "rhs", "leaf"), P("leaf"), P("leaf"), P(), P(), P())
    return jax.shard_map(
        per_device, mesh=mesh, in_specs=in_specs, out_specs=P(None, "rhs", "leaf"), check_vma=False
    )
```

```python
import functools
import jax
import jax.numpy as jnp
from jax import lax
from jax.experimental import pallas as pl
from jax.experimental.pallas import tpu as pltpu
from jax.sharding import PartitionSpec as P

LANES = 256
CHUNKS = 2
UNROLL = 8
GROUP = 8
VMEM_BYTES = 56 * 1024 * 1024


def dot_rows(left, right):
    return lax.dot_general(
        left, right, (((1,), (1,)), ((), ())), preferred_element_type=jnp.float32
    )


def level_matrix(transfer_ref, level, halves):
    rank = transfer_ref.shape[4]
    for part in range(2):
        for child in range(2):
            halves[part, child] = transfer_ref[level, part, child].astype(jnp.float32)
    rows = []
    for child in range(2):
        real_0, real_1 = (halves[0, child, pl.ds(half, rank, stride=2), :] for half in range(2))
        imag_0, imag_1 = (halves[1, child, pl.ds(half, rank, stride=2), :] for half in range(2))
        rows.append(jnp.concatenate([real_0, -imag_0, real_1, -imag_1], axis=1))
        rows.append(jnp.concatenate([imag_0, real_0, imag_1, real_1], axis=1))
    return jnp.concatenate(rows, axis=0).astype(jnp.bfloat16)


def leaf_matrix(basis_ref):
    real, imag = basis_ref[0], basis_ref[1]
    zero = jnp.zeros_like(real)
    rows = [
        jnp.concatenate([real, zero, -imag, zero], axis=1),
        jnp.concatenate([imag, zero, real, zero], axis=1),
        jnp.concatenate([zero, real, zero, -imag], axis=1),
        jnp.concatenate([zero, imag, zero, real], axis=1),
    ]
    return jnp.concatenate(rows, axis=0)


def eval_matrix(basis_ref):
    real, imag = basis_ref[0], basis_ref[1]
    zero = jnp.zeros_like(real)
    rows = [
        jnp.concatenate([real, -imag, zero, zero], axis=1),
        jnp.concatenate([zero, zero, real, -imag], axis=1),
        jnp.concatenate([imag, real, zero, zero], axis=1),
        jnp.concatenate([zero, zero, imag, real], axis=1),
    ]
    return jnp.concatenate(rows, axis=0)


def pair_up(state, targets, vecs):
    rows, width = state.shape
    block = targets * vecs
    if block % 16:
        state = state.astype(jnp.float32)
    split = state.reshape(rows // (2 * block), 2, block, width)
    joined = jnp.concatenate([split[:, 0], split[:, 1]], axis=-1)
    return joined.reshape(rows // 2, 2 * width).astype(jnp.bfloat16)


def children(result, vecs):
    rows, width = result.shape
    half = width // 2
    blocks = result.reshape(rows // vecs, vecs, width)
    stacked = jnp.stack([blocks[..., :half], blocks[..., half:]], axis=1)
    return stacked.reshape(rows * 2, half).astype(jnp.bfloat16)


def one_hot(order_block):
    low = jnp.bitwise_and(order_block, LANES - 1)
    rows = lax.broadcasted_iota(jnp.int32, (LANES, order_block.shape[1]), 0)
    return jnp.where(rows == low, 1.0, 0.0).astype(jnp.bfloat16)


def aligned(index, size):
    return pl.ds(pl.multiple_of(index * size, size), size)


def weigh(exc_ref, weight_ref, weighted):
    vecs, points = exc_ref.shape[1:]
    for block in range(points // LANES):
        lanes = pl.ds(block * LANES, LANES)
        scaled = [
            exc_ref[part, :, lanes].astype(jnp.float32) * weight_ref[:, lanes] for part in range(2)
        ]
        weighted[pl.ds(block * 2 * vecs, 2 * vecs), :] = jnp.concatenate(scaled, axis=0).astype(
            jnp.bfloat16
        )


def gather_step(step, vecs, blocks, order_ref, weighted, hot, pairs):
    half = LANES // 2
    order = order_ref[:, aligned(step, LANES)]
    table = one_hot(order)
    hot[step] = table
    spread = jnp.dot(weighted[...], table, preferred_element_type=jnp.float32)
    high = jnp.broadcast_to(lax.shift_right_logical(order, 8), (vecs, LANES))
    real, imag = spread[:vecs], spread[vecs : 2 * vecs]
    for block in range(1, blocks):
        here = high == block
        base = block * 2 * vecs
        real = jnp.where(here, spread[base : base + vecs], real)
        imag = jnp.where(here, spread[base + vecs : base + 2 * vecs], imag)
    rows = [
        jnp.concatenate([real[:, lo : lo + half], imag[:, lo : lo + half]], axis=1)
        for lo in (0, half)
    ]
    pairs[aligned(step, 2 * vecs), :] = jnp.concatenate(rows, axis=0).astype(jnp.bfloat16)


def scatter_steps(group, vecs, blocks, count, order_ref, hot, values, total):
    half = LANES // 2
    spreads, tables = [], []
    for inner in range(count):
        step = group * count + inner
        order = order_ref[:, aligned(step, LANES)]
        held = values[aligned(step, 2 * vecs), :]
        real, imag = (
            jnp.concatenate([held[:vecs, lo : lo + half], held[vecs:, lo : lo + half]], axis=1)
            for lo in (0, half)
        )
        high = jnp.broadcast_to(lax.shift_right_logical(order, 8), (vecs, LANES))
        rows = []
        for block in range(blocks):
            here = high == block
            rows.append(jnp.where(here, real, 0.0))
            rows.append(jnp.where(here, imag, 0.0))
        spreads.append(jnp.concatenate(rows, axis=0).astype(jnp.bfloat16))
        tables.append(hot[step])
    total[...] += dot_rows(jnp.concatenate(spreads, axis=1), jnp.concatenate(tables, axis=1))


def write_out(vecs, blocks, total, out_ref):
    for block in range(blocks):
        rows = block * 2 * vecs
        for part in range(2):
            held = total[pl.ds(rows + part * vecs, vecs), :]
            out_ref[part, :, pl.ds(block * LANES, LANES)] = held.astype(out_ref.dtype)


def merge(vecs, group, held, hot, far_mats, order_ref, out_ref, values, total):
    blocks = order_ref.shape[1] // LANES
    count, sources, rows, width = held.shape
    targets = rows // vecs
    far_levels = far_mats.shape[0] - 1
    state = held[...].reshape(count * sources * rows, width)
    for level in range(far_levels):
        state = children(dot_rows(pair_up(state, targets, vecs), far_mats[level]), vecs)
        targets *= 2
    values[...] = dot_rows(pair_up(state, 1, vecs), far_mats[far_levels])

    def scatter(step, carry):
        scatter_steps(step, vecs, blocks, group, order_ref, hot, values, total)
        return carry

    lax.fori_loop(0, blocks // group, scatter, 0)
    write_out(vecs, blocks, total, out_ref)


def fused_kernel(count, chunks, near_levels, unroll, group, exc_hbm, weight_hbm, order_hbm, leaf_hbm,
                transfer_hbm, eval_hbm, out_ref, held, hot, far_mats, exc_ref, weight_ref,
                order_ref, leaf_ref, transfer_ref, eval_ref, weighted, pairs, mats, halves, sent, values,
                total, load_sems, send_sems, recv_sems):
    vecs, points = exc_ref.shape[1:]
    levels = transfer_ref.shape[0]
    blocks = points // LANES
    loads = [
        pltpu.make_async_copy(source, target, load_sems.at[index])
        for index, (source, target) in enumerate(
            [
                (exc_hbm, exc_ref),
                (weight_hbm, weight_ref),
                (order_hbm, order_ref),
                (transfer_hbm, transfer_ref),
                (leaf_hbm, leaf_ref),
                (eval_hbm, eval_ref),
            ]
        )
    ]
    for load in loads:
        load.start()
    me = lax.axis_index("leaf")
    peers = [(hop, lax.rem(me + hop, count)) for hop in range(1, count)]
    barrier = pltpu.get_barrier_semaphore()
    for hop, peer in peers:
        pl.semaphore_signal(
            barrier, inc=1, device_id={"leaf": peer}, device_id_type=pl.DeviceIdType.MESH
        )
    steps = blocks // chunks
    unroll = min(unroll, steps)
    groups = steps // unroll
    inside = near_levels // groups
    loads[0].wait()
    loads[1].wait()
    weigh(exc_ref, weight_ref, weighted)
    for load in loads[2:]:
        load.wait()
    for level in range(inside * groups, near_levels):
        mats[level] = level_matrix(transfer_ref, level, halves.at[0])
    mats[near_levels] = leaf_matrix(leaf_ref)
    sources, rows, width = held.shape[1:]
    sources //= chunks
    copies = []
    for chunk in range(chunks):

        def gather(round, carry):
            for inner in range(unroll):
                step = chunk * steps + round * unroll + inner
                gather_step(step, vecs, blocks, order_ref, weighted, hot, pairs)
                if chunk == 0 and inner < inside:
                    level = round * inside + inner
                    mats[level] = level_matrix(transfer_ref, level, halves.at[inner % 2])
            return carry

        lax.fori_loop(0, groups, gather, 0)
        start = chunk * steps * 2 * vecs
        joined = dot_rows(pairs[start : start + steps * 2 * vecs, :], mats[near_levels]).astype(
            jnp.bfloat16
        )
        for level in range(near_levels):
            state = children(dot_rows(joined, mats[level]), vecs)
            if level + 1 < near_levels:
                joined = pair_up(state, 2 << level, vecs)
        state = state.reshape(sources, count, rows, width)
        for peer in range(count):
            sent[chunk, peer] = state[:, peer]
        if chunk == 0:
            pl.semaphore_wait(barrier, count - 1)
        for hop, peer in peers:
            copy = pltpu.make_async_remote_copy(
                src_ref=sent.at[chunk, peer],
                dst_ref=held.at[me, pl.ds(chunk * sources, sources)],
                send_sem=send_sems.at[chunk, hop],
                recv_sem=recv_sems.at[chunk, hop],
                device_id={"leaf": peer},
                device_id_type=pl.DeviceIdType.MESH,
            )
            copy.start()
            copies.append(copy)
        held[me, chunk * sources : (chunk + 1) * sources] = sent[chunk, me]
    for level in range(near_levels, levels):
        far_mats[level - near_levels] = level_matrix(transfer_ref, level, halves.at[level % 2])
    far_mats[levels - near_levels] = eval_matrix(eval_ref)
    total[...] = jnp.zeros_like(total)
    for copy in copies:
        copy.wait()
    merge(vecs, group, held, hot, far_mats, order_ref, out_ref, values, total)


def near_kernel(near_levels, exc_ref, weight_ref, order_ref, leaf_ref, transfer_ref,
                out_ref, weighted, hot, pairs, halves):
    vecs, points = exc_ref.shape[1:]
    blocks = points // LANES
    weigh(exc_ref, weight_ref, weighted)

    def gather(step, carry):
        gather_step(step, vecs, blocks, order_ref, weighted, hot, pairs)
        return carry

    lax.fori_loop(0, blocks, gather, 0)
    joined = dot_rows(pairs[...], leaf_matrix(leaf_ref)).astype(jnp.bfloat16)
    for level in range(near_levels):
        state = children(dot_rows(joined, level_matrix(transfer_ref, level, halves)), vecs)
        if level + 1 < near_levels:
            joined = pair_up(state, 2 << level, vecs)
    out_ref[...] = state


def far_kernel(near_levels, per_peer, vecs, state_ref, order_ref, transfer_ref, eval_ref,
               out_ref, hot, values, total, halves):
    blocks = order_ref.shape[1] // LANES
    state = state_ref[...]
    targets = per_peer
    for level in range(near_levels, transfer_ref.shape[0]):
        matrix = level_matrix(transfer_ref, level, halves)
        state = children(dot_rows(pair_up(state, targets, vecs), matrix), vecs)
        targets *= 2
    values[...] = dot_rows(pair_up(state, 1, vecs), eval_matrix(eval_ref))
    total[...] = jnp.zeros_like(total)

    def scatter(step, carry):
        hot[step] = one_hot(order_ref[:, aligned(step, LANES)])
        scatter_steps(step, vecs, blocks, 1, order_ref, hot, values, total)
        return carry

    lax.fori_loop(0, blocks, scatter, 0)
    write_out(vecs, blocks, total, out_ref)


def per_device(excitation, source_weight, tree_order, leaf_basis, transfer, eval_basis):
    vecs, points = excitation.shape[1:]
    levels, rank = transfer.shape[0], leaf_basis.shape[1]
    leaf_size = leaf_basis.shape[2]
    boxes = points // leaf_size
    blocks = points // LANES
    count = lax.axis_size("leaf")
    transfer = transfer.reshape(levels, 2, 2, 2 * rank, rank)
    weight_row = source_weight.reshape(1, points)
    order_row = tree_order.reshape(1, points)
    box_levels = boxes.bit_length() - 1
    out_shape = jax.ShapeDtypeStruct((2, vecs, points), jnp.float32)
    weighted = pltpu.VMEM((blocks * 2 * vecs, LANES), jnp.bfloat16)
    pairs = pltpu.VMEM((boxes * vecs // 2, 4 * rank), jnp.bfloat16)
    values = pltpu.VMEM((boxes * vecs // 2, 4 * rank), jnp.float32)
    total = pltpu.VMEM((blocks * 2 * vecs, LANES), jnp.float32)
    hot = pltpu.VMEM((blocks, LANES, LANES), jnp.bfloat16)
    halves = pltpu.VMEM((2, 2, 2 * rank, rank), jnp.float32)
    near_levels = (16 * count // vecs).bit_length() - 1
    chunks = CHUNKS
    while chunks > 1 and boxes // chunks < 1 << near_levels:
        chunks //= 2
    if near_levels < box_levels:
        sources = boxes >> near_levels
        rows = boxes * vecs // (count * sources)
        far_count = levels - near_levels + 1
        return pl.pallas_call(
            functools.partial(fused_kernel, count, chunks, near_levels, UNROLL, min(GROUP, blocks)),
            out_shape=jax.ShapeDtypeStruct((2, vecs, points), jnp.bfloat16),
            in_specs=[pl.BlockSpec(memory_space=pltpu.HBM)] * 6,
            out_specs=pl.BlockSpec(memory_space=pltpu.VMEM),
            scratch_shapes=[
                pltpu.VMEM((count, sources, rows, 2 * rank), jnp.bfloat16),
                hot,
                pltpu.VMEM((far_count, 4 * rank, 4 * rank), jnp.bfloat16),
                pltpu.VMEM(excitation.shape, excitation.dtype),
                pltpu.VMEM(weight_row.shape, weight_row.dtype),
                pltpu.VMEM(order_row.shape, order_row.dtype),
                pltpu.VMEM(leaf_basis.shape, leaf_basis.dtype),
                pltpu.VMEM(transfer.shape, transfer.dtype),
                pltpu.VMEM(eval_basis.shape, eval_basis.dtype),
                weighted,
                pairs,
                pltpu.VMEM((near_levels + 1, 4 * rank, 4 * rank), jnp.bfloat16),
                pltpu.VMEM((2, 2, 2, 2 * rank, rank), jnp.float32),
                pltpu.VMEM((chunks, count, sources // chunks, rows, 2 * rank), jnp.bfloat16),
                values,
                total,
                pltpu.SemaphoreType.DMA((6,)),
                pltpu.SemaphoreType.DMA((chunks, count)),
                pltpu.SemaphoreType.DMA((chunks, count)),
            ],
            compiler_params=pltpu.CompilerParams(
                vmem_limit_bytes=VMEM_BYTES, collective_id=0, has_side_effects=True
            ),
            name="fused",
        )(excitation, weight_row, order_row, leaf_basis, transfer, eval_basis).astype(jnp.float32)
    params = pltpu.CompilerParams(vmem_limit_bytes=VMEM_BYTES)
    state = pl.pallas_call(
        functools.partial(near_kernel, box_levels),
        out_shape=jax.ShapeDtypeStruct((boxes * vecs, 2 * rank), jnp.bfloat16),
        scratch_shapes=[weighted, hot, pairs, halves],
        compiler_params=params,
        name="near",
    )(excitation, weight_row, order_row, leaf_basis, transfer)
    state = lax.all_to_all(state, "leaf", split_axis=0, concat_axis=0, tiled=True)
    return pl.pallas_call(
        functools.partial(far_kernel, box_levels, boxes // count, vecs),
        out_shape=out_shape,
        scratch_shapes=[hot, values, total, halves],
        compiler_params=params,
        name="far",
    )(state, order_row, transfer, eval_basis)


def solution(mesh):
    in_specs = (P(None, "rhs", "leaf"), P("leaf"), P("leaf"), P(), P(), P())
    return jax.shard_map(
        per_device, mesh=mesh, in_specs=in_specs, out_specs=P(None, "rhs", "leaf"), check_vma=False
    )
```

```python
import functools
import jax
import jax.numpy as jnp
from jax import lax
from jax.experimental import pallas as pl
from jax.experimental.pallas import tpu as pltpu
from jax.sharding import PartitionSpec as P

LANES = 256
CHUNKS = 2
UNROLL = 8
GROUP = 16
VMEM_BYTES = 56 * 1024 * 1024


def dot_rows(left, right):
    return lax.dot_general(
        left, right, (((1,), (1,)), ((), ())), preferred_element_type=jnp.float32
    )


def level_matrix(transfer_ref, level, halves):
    rank = transfer_ref.shape[4]
    for part in range(2):
        for child in range(2):
            halves[part, child] = transfer_ref[level, part, child].astype(jnp.float32)
    rows = []
    for child in range(2):
        real_0, real_1 = (halves[0, child, pl.ds(half, rank, stride=2), :] for half in range(2))
        imag_0, imag_1 = (halves[1, child, pl.ds(half, rank, stride=2), :] for half in range(2))
        rows.append(jnp.concatenate([real_0, -imag_0, real_1, -imag_1], axis=1))
        rows.append(jnp.concatenate([imag_0, real_0, imag_1, real_1], axis=1))
    return jnp.concatenate(rows, axis=0).astype(jnp.bfloat16)


def leaf_matrix(basis_ref):
    real, imag = basis_ref[0], basis_ref[1]
    zero = jnp.zeros_like(real)
    rows = [
        jnp.concatenate([real, zero, -imag, zero], axis=1),
        jnp.concatenate([imag, zero, real, zero], axis=1),
        jnp.concatenate([zero, real, zero, -imag], axis=1),
        jnp.concatenate([zero, imag, zero, real], axis=1),
    ]
    return jnp.concatenate(rows, axis=0)


def eval_matrix(basis_ref):
    real, imag = basis_ref[0], basis_ref[1]
    zero = jnp.zeros_like(real)
    rows = [
        jnp.concatenate([real, -imag, zero, zero], axis=1),
        jnp.concatenate([zero, zero, real, -imag], axis=1),
        jnp.concatenate([imag, real, zero, zero], axis=1),
        jnp.concatenate([zero, zero, imag, real], axis=1),
    ]
    return jnp.concatenate(rows, axis=0)


def pair_up(state, targets, vecs):
    rows, width = state.shape
    block = targets * vecs
    if block % 16:
        state = state.astype(jnp.float32)
    split = state.reshape(rows // (2 * block), 2, block, width)
    joined = jnp.concatenate([split[:, 0], split[:, 1]], axis=-1)
    return joined.reshape(rows // 2, 2 * width).astype(jnp.bfloat16)


def children(result, vecs):
    rows, width = result.shape
    half = width // 2
    blocks = result.reshape(rows // vecs, vecs, width)
    stacked = jnp.stack([blocks[..., :half], blocks[..., half:]], axis=1)
    return stacked.reshape(rows * 2, half).astype(jnp.bfloat16)


def one_hot(order_block):
    low = jnp.bitwise_and(order_block, LANES - 1)
    rows = lax.broadcasted_iota(jnp.int32, (LANES, order_block.shape[1]), 0)
    return jnp.where(rows == low, 1.0, 0.0).astype(jnp.bfloat16)


def aligned(index, size):
    return pl.ds(pl.multiple_of(index * size, size), size)


def weigh(exc_ref, weight_ref, weighted):
    vecs, points = exc_ref.shape[1:]
    for block in range(points // LANES):
        lanes = pl.ds(block * LANES, LANES)
        scaled = [
            exc_ref[part, :, lanes].astype(jnp.float32) * weight_ref[:, lanes] for part in range(2)
        ]
        weighted[pl.ds(block * 2 * vecs, 2 * vecs), :] = jnp.concatenate(scaled, axis=0).astype(
            jnp.bfloat16
        )


def gather_step(step, vecs, blocks, order_ref, weighted, hot, pairs):
    half = LANES // 2
    order = order_ref[:, aligned(step, LANES)]
    table = one_hot(order)
    hot[step] = table
    spread = jnp.dot(weighted[...], table, preferred_element_type=jnp.float32)
    high = jnp.broadcast_to(lax.shift_right_logical(order, 8), (vecs, LANES))
    real, imag = spread[:vecs], spread[vecs : 2 * vecs]
    for block in range(1, blocks):
        here = high == block
        base = block * 2 * vecs
        real = jnp.where(here, spread[base : base + vecs], real)
        imag = jnp.where(here, spread[base + vecs : base + 2 * vecs], imag)
    rows = [
        jnp.concatenate([real[:, lo : lo + half], imag[:, lo : lo + half]], axis=1)
        for lo in (0, half)
    ]
    pairs[aligned(step, 2 * vecs), :] = jnp.concatenate(rows, axis=0).astype(jnp.bfloat16)


def scatter_steps(group, vecs, blocks, count, order_ref, hot, values, total):
    half = LANES // 2
    spreads, tables = [], []
    for inner in range(count):
        step = group * count + inner
        order = order_ref[:, aligned(step, LANES)]
        held = values[aligned(step, 2 * vecs), :]
        real, imag = (
            jnp.concatenate([held[:vecs, lo : lo + half], held[vecs:, lo : lo + half]], axis=1)
            for lo in (0, half)
        )
        high = jnp.broadcast_to(lax.shift_right_logical(order, 8), (vecs, LANES))
        rows = []
        for block in range(blocks):
            here = high == block
            rows.append(jnp.where(here, real, 0.0))
            rows.append(jnp.where(here, imag, 0.0))
        spreads.append(jnp.concatenate(rows, axis=0).astype(jnp.bfloat16))
        tables.append(hot[step])
    total[...] += dot_rows(jnp.concatenate(spreads, axis=1), jnp.concatenate(tables, axis=1))


def write_out(vecs, blocks, total, out_ref):
    for block in range(blocks):
        rows = block * 2 * vecs
        for part in range(2):
            held = total[pl.ds(rows + part * vecs, vecs), :]
            out_ref[part, :, pl.ds(block * LANES, LANES)] = held.astype(out_ref.dtype)


def merge(vecs, group, held, hot, far_mats, order_ref, out_ref, values, total):
    blocks = order_ref.shape[1] // LANES
    count, sources, rows, width = held.shape
    targets = rows // vecs
    far_levels = far_mats.shape[0] - 1
    state = held[...].reshape(count * sources * rows, width)
    for level in range(far_levels):
        state = children(dot_rows(pair_up(state, targets, vecs), far_mats[level]), vecs)
        targets *= 2
    values[...] = dot_rows(pair_up(state, 1, vecs), far_mats[far_levels])

    def scatter(step, carry):
        scatter_steps(step, vecs, blocks, group, order_ref, hot, values, total)
        return carry

    lax.fori_loop(0, blocks // group, scatter, 0)
    write_out(vecs, blocks, total, out_ref)


def fused_kernel(count, chunks, near_levels, unroll, group, exc_hbm, weight_hbm, order_hbm, leaf_hbm,
                transfer_hbm, eval_hbm, out_ref, held, hot, far_mats, exc_ref, weight_ref,
                order_ref, leaf_ref, transfer_ref, eval_ref, weighted, pairs, mats, halves, sent, values,
                total, load_sems, send_sems, recv_sems):
    vecs, points = exc_ref.shape[1:]
    levels = transfer_ref.shape[0]
    blocks = points // LANES
    loads = [
        pltpu.make_async_copy(source, target, load_sems.at[index])
        for index, (source, target) in enumerate(
            [
                (exc_hbm, exc_ref),
                (weight_hbm, weight_ref),
                (order_hbm, order_ref),
                (transfer_hbm, transfer_ref),
                (leaf_hbm, leaf_ref),
                (eval_hbm, eval_ref),
            ]
        )
    ]
    for load in loads:
        load.start()
    me = lax.axis_index("leaf")
    peers = [(hop, lax.rem(me + hop, count)) for hop in range(1, count)]
    barrier = pltpu.get_barrier_semaphore()
    for hop, peer in peers:
        pl.semaphore_signal(
            barrier, inc=1, device_id={"leaf": peer}, device_id_type=pl.DeviceIdType.MESH
        )
    steps = blocks // chunks
    unroll = min(unroll, steps)
    groups = steps // unroll
    inside = min(near_levels, unroll)
    loads[0].wait()
    loads[1].wait()
    weigh(exc_ref, weight_ref, weighted)
    loads[2].wait()
    sources, rows, width = held.shape[1:]
    sources //= chunks
    copies = []
    for chunk in range(chunks):

        def gather(round, build):
            for inner in range(unroll):
                step = chunk * steps + round * unroll + inner
                gather_step(step, vecs, blocks, order_ref, weighted, hot, pairs)
                if build and inner < inside:
                    mats[inner] = level_matrix(transfer_ref, inner, halves.at[inner % 2])

        def gather_round(round, carry):
            gather(round, False)
            return carry

        if chunk == 0:
            lax.fori_loop(0, groups - 1, gather_round, 0)
            for load in loads[3:]:
                load.wait()
            mats[near_levels] = leaf_matrix(leaf_ref)
            gather(groups - 1, True)
            for level in range(inside, near_levels):
                mats[level] = level_matrix(transfer_ref, level, halves.at[0])
        else:
            lax.fori_loop(0, groups, gather_round, 0)
        start = chunk * steps * 2 * vecs
        joined = dot_rows(pairs[start : start + steps * 2 * vecs, :], mats[near_levels]).astype(
            jnp.bfloat16
        )
        for level in range(near_levels):
            state = children(dot_rows(joined, mats[level]), vecs)
            if level + 1 < near_levels:
                joined = pair_up(state, 2 << level, vecs)
        state = state.reshape(sources, count, rows, width)
        for peer in range(count):
            sent[chunk, peer] = state[:, peer]
        if chunk == 0:
            pl.semaphore_wait(barrier, count - 1)
        for hop, peer in peers:
            copy = pltpu.make_async_remote_copy(
                src_ref=sent.at[chunk, peer],
                dst_ref=held.at[me, pl.ds(chunk * sources, sources)],
                send_sem=send_sems.at[chunk, hop],
                recv_sem=recv_sems.at[chunk, hop],
                device_id={"leaf": peer},
                device_id_type=pl.DeviceIdType.MESH,
            )
            copy.start()
            copies.append(copy)
        held[me, chunk * sources : (chunk + 1) * sources] = sent[chunk, me]
    for level in range(near_levels, levels):
        far_mats[level - near_levels] = level_matrix(transfer_ref, level, halves.at[level % 2])
    far_mats[levels - near_levels] = eval_matrix(eval_ref)
    total[...] = jnp.zeros_like(total)
    for copy in copies:
        copy.wait()
    merge(vecs, group, held, hot, far_mats, order_ref, out_ref, values, total)


def near_kernel(near_levels, exc_ref, weight_ref, order_ref, leaf_ref, transfer_ref,
                out_ref, weighted, hot, pairs, halves):
    vecs, points = exc_ref.shape[1:]
    blocks = points // LANES
    weigh(exc_ref, weight_ref, weighted)

    def gather(step, carry):
        gather_step(step, vecs, blocks, order_ref, weighted, hot, pairs)
        return carry

    lax.fori_loop(0, blocks, gather, 0)
    joined = dot_rows(pairs[...], leaf_matrix(leaf_ref)).astype(jnp.bfloat16)
    for level in range(near_levels):
        state = children(dot_rows(joined, level_matrix(transfer_ref, level, halves)), vecs)
        if level + 1 < near_levels:
            joined = pair_up(state, 2 << level, vecs)
    out_ref[...] = state


def far_kernel(near_levels, per_peer, vecs, state_ref, order_ref, transfer_ref, eval_ref,
               out_ref, hot, values, total, halves):
    blocks = order_ref.shape[1] // LANES
    state = state_ref[...]
    targets = per_peer
    for level in range(near_levels, transfer_ref.shape[0]):
        matrix = level_matrix(transfer_ref, level, halves)
        state = children(dot_rows(pair_up(state, targets, vecs), matrix), vecs)
        targets *= 2
    values[...] = dot_rows(pair_up(state, 1, vecs), eval_matrix(eval_ref))
    total[...] = jnp.zeros_like(total)

    def scatter(step, carry):
        hot[step] = one_hot(order_ref[:, aligned(step, LANES)])
        scatter_steps(step, vecs, blocks, 1, order_ref, hot, values, total)
        return carry

    lax.fori_loop(0, blocks, scatter, 0)
    write_out(vecs, blocks, total, out_ref)


def per_device(excitation, source_weight, tree_order, leaf_basis, transfer, eval_basis):
    vecs, points = excitation.shape[1:]
    levels, rank = transfer.shape[0], leaf_basis.shape[1]
    leaf_size = leaf_basis.shape[2]
    boxes = points // leaf_size
    blocks = points // LANES
    count = lax.axis_size("leaf")
    transfer = transfer.reshape(levels, 2, 2, 2 * rank, rank)
    weight_row = source_weight.reshape(1, points)
    order_row = tree_order.reshape(1, points)
    box_levels = boxes.bit_length() - 1
    out_shape = jax.ShapeDtypeStruct((2, vecs, points), jnp.float32)
    weighted = pltpu.VMEM((blocks * 2 * vecs, LANES), jnp.bfloat16)
    pairs = pltpu.VMEM((boxes * vecs // 2, 4 * rank), jnp.bfloat16)
    values = pltpu.VMEM((boxes * vecs // 2, 4 * rank), jnp.float32)
    total = pltpu.VMEM((blocks * 2 * vecs, LANES), jnp.float32)
    hot = pltpu.VMEM((blocks, LANES, LANES), jnp.bfloat16)
    halves = pltpu.VMEM((2, 2, 2 * rank, rank), jnp.float32)
    near_levels = (16 * count // vecs).bit_length() - 1
    chunks = CHUNKS
    while chunks > 1 and boxes // chunks < 1 << near_levels:
        chunks //= 2
    if near_levels < box_levels:
        sources = boxes >> near_levels
        rows = boxes * vecs // (count * sources)
        far_count = levels - near_levels + 1
        return pl.pallas_call(
            functools.partial(fused_kernel, count, chunks, near_levels, UNROLL, min(GROUP, blocks)),
            out_shape=jax.ShapeDtypeStruct((2, vecs, points), jnp.bfloat16),
            in_specs=[pl.BlockSpec(memory_space=pltpu.HBM)] * 6,
            out_specs=pl.BlockSpec(memory_space=pltpu.VMEM),
            scratch_shapes=[
                pltpu.VMEM((count, sources, rows, 2 * rank), jnp.bfloat16),
                hot,
                pltpu.VMEM((far_count, 4 * rank, 4 * rank), jnp.bfloat16),
                pltpu.VMEM(excitation.shape, excitation.dtype),
                pltpu.VMEM(weight_row.shape, weight_row.dtype),
                pltpu.VMEM(order_row.shape, order_row.dtype),
                pltpu.VMEM(leaf_basis.shape, leaf_basis.dtype),
                pltpu.VMEM(transfer.shape, transfer.dtype),
                pltpu.VMEM(eval_basis.shape, eval_basis.dtype),
                weighted,
                pairs,
                pltpu.VMEM((near_levels + 1, 4 * rank, 4 * rank), jnp.bfloat16),
                pltpu.VMEM((2, 2, 2, 2 * rank, rank), jnp.float32),
                pltpu.VMEM((chunks, count, sources // chunks, rows, 2 * rank), jnp.bfloat16),
                values,
                total,
                pltpu.SemaphoreType.DMA((6,)),
                pltpu.SemaphoreType.DMA((chunks, count)),
                pltpu.SemaphoreType.DMA((chunks, count)),
            ],
            compiler_params=pltpu.CompilerParams(
                vmem_limit_bytes=VMEM_BYTES, collective_id=0, has_side_effects=True
            ),
            name="fused",
        )(excitation, weight_row, order_row, leaf_basis, transfer, eval_basis).astype(jnp.float32)
    params = pltpu.CompilerParams(vmem_limit_bytes=VMEM_BYTES)
    state = pl.pallas_call(
        functools.partial(near_kernel, box_levels),
        out_shape=jax.ShapeDtypeStruct((boxes * vecs, 2 * rank), jnp.bfloat16),
        scratch_shapes=[weighted, hot, pairs, halves],
        compiler_params=params,
        name="near",
    )(excitation, weight_row, order_row, leaf_basis, transfer)
    state = lax.all_to_all(state, "leaf", split_axis=0, concat_axis=0, tiled=True)
    return pl.pallas_call(
        functools.partial(far_kernel, box_levels, boxes // count, vecs),
        out_shape=out_shape,
        scratch_shapes=[hot, values, total, halves],
        compiler_params=params,
        name="far",
    )(state, order_row, transfer, eval_basis)


def solution(mesh):
    in_specs = (P(None, "rhs", "leaf"), P("leaf"), P("leaf"), P(), P(), P())
    return jax.shard_map(
        per_device, mesh=mesh, in_specs=in_specs, out_specs=P(None, "rhs", "leaf"), check_vma=False
    )
```
